1024 devices in a mesh: occ: 16 (over x_lo, y, core), vir: 64 (over z, x_hi).
Axes of the slice: x: 4 (x_hi: 2, x_lo: 2; x = x_hi * 2 + x_lo), y: 4, z: 32, core: 2. Of those that a mesh axis runs over, the one named last changes fastest.
Arguments:
- amplitudes: bfloat16 [1600, 98304], P('occ', 'vir'), may hold values from -6 to 6
- integrals: bfloat16 [98304, 8192], P('vir', 'occ'), may hold values from -0.078125 to 0.078125
- block_sizes: int32 [64], replicated, may hold values from 1 to 1536, 49152 in all
Outputs:
- residual: float32 [8192, 1600], P(('occ', 'vir'))
The draws below stay inside these ranges and needn't reach their ends.
Inputs may be any that keep to these rules, and one draw needn't show every extreme that they name: `block_sizes`: block sizes sum to 49152; at least one block is full.
All inputs are finite; a program needn't handle non-finite values.
Results may differ from the reference program's by a relative error of at most 0.0003.
Values may be sent and summed in bfloat16 or wider, within the bound.
A program may use at most 32 MiB of HBM per device.

```python
import math
import jax
import jax.numpy as jnp
import numpy as np
from jax import lax

IJ = 1600
CD_DEV = 1536
CD = 98304
AB = 8192
LIVE_TOTAL = 49152
N_VIR = 64


def strengthened(drawn, rng, source, target, parts, factor):
    def block_of(dim):
        return (jnp.arange(drawn.shape[dim]) // (drawn.shape[dim] // parts)).reshape((-1,) + (1,) * (drawn.ndim - 1 - dim))

    one_side = jax.random.permutation(rng, parts)[block_of(target)]
    other_side = (block_of(target) + parts // 2) % parts
    return jnp.where((block_of(source) == one_side) | (block_of(source) == other_side), factor * drawn, drawn)


def shard_levels(key, extent, split, least, largest):
    def one(position, parts):
        heights = jax.random.uniform(jax.random.fold_in(jax.random.fold_in(key, 6), position), (parts,), jnp.float32, least / len(split), largest / len(split))
        return jnp.repeat(jnp.exp(heights), extent[position] // parts).reshape((-1,) + (1,) * (len(extent) - position - 1))

    level = one(*split[0])
    for cut in split[1:]:
        level = level * one(*cut)
    return level


def profile(amount, total, bound, skew):
    weights = [(1 << 20) // math.isqrt(grade ** skew) + 1 for grade in range(2, amount + 1)]
    rest, counts = total - bound - (amount - 1), [1] * (amount - 1)
    while rest > 0:
        movable = [i for i in range(amount - 1) if counts[i] < bound]
        whole, remaining = sum([weights[i] for i in movable]), rest
        for i in movable:
            extra = min(bound - counts[i], max(1, remaining * weights[i] // whole), rest)
            counts[i] = counts[i] + extra
            rest = rest - extra
    return np.array([bound] + counts)


def uneven_parts(rng, count, total, reach, skew):
    if count == 2:
        one = jax.random.randint(rng, (), max(1, total - reach), min(reach, total - 1) + 1)
        return jnp.stack([one, total - one])
    sizes = jnp.asarray(profile(count, total, reach, skew), jnp.int32)
    pairs = (count - 1) // 2
    giver, sink = sizes[1:1 + 2 * pairs:2], sizes[2:2 + 2 * pairs:2]
    room = jnp.minimum(giver - 1, reach - sink)
    moved = jax.random.randint(jax.random.fold_in(rng, 1), (pairs,), 0, 1 << 20) % (room + 1)
    sizes = sizes.at[1:1 + 2 * pairs:2].set(giver - moved).at[2:2 + 2 * pairs:2].set(sink + moved)
    return sizes[jax.random.permutation(jax.random.fold_in(rng, 2), count)]


def bell_draw(stream_key, dims, scale, most, pieces=(), kind=jnp.bfloat16):
    values = jax.random.normal(stream_key, dims, jnp.float32) * scale
    if len(pieces) > 0:
        values = shard_levels(stream_key, dims, pieces, -0.22, 0.18) * values
    return jnp.clip(values, min=-most, max=most).astype(kind)


def bell_draw_with(stream_key, extent, scale, reach, cuts, heavy, held_as=jnp.bfloat16):
    array = scale * jax.random.normal(stream_key, extent, jnp.float32)
    if cuts:
        array = array * shard_levels(stream_key, extent, cuts, -0.22, 0.18)
    return jnp.clip(strengthened(array, jax.random.fold_in(stream_key, 3), *heavy), -reach, reach).astype(held_as)


def setup_inputs(seed: int = 0) -> dict:
    seeds = jax.random.split(jax.random.key(seed), 4)
    amplitudes = bell_draw(seeds[0], (IJ, CD), 1.0, 6.0, ((0, 16), (1, 64)))
    integrals = bell_draw_with(seeds[1], (CD, AB), (CD // 2) ** -0.5, 0.078125, ((0, 64), (1, 16)), (0, 1, 64, 4.0))
    block_sizes = uneven_parts(seeds[2], N_VIR, LIVE_TOTAL, CD_DEV, 2).astype(jnp.int32)
    return {"amplitudes": amplitudes, "integrals": integrals, "block_sizes": block_sizes}


def reference(amplitudes, integrals, block_sizes):
    rows = jnp.arange(CD, dtype=jnp.int32)
    limit = jnp.repeat(block_sizes, CD_DEV)
    live = (rows % CD_DEV) < limit
    masked = jnp.where(live[:, None], integrals, jnp.zeros_like(integrals))
    return lax.dot_general(masked, amplitudes, (((0,), (1,)), ((), ())), preferred_element_type=jnp.float32)
```

```python
import jax
import jax.numpy as jnp
from jax import lax
from jax.experimental import pallas as pl
from jax.experimental.pallas import tpu as pltpu
from jax.sharding import PartitionSpec as P

MESH = pl.DeviceIdType.MESH
F32, BF16, I16 = jnp.float32, jnp.bfloat16, jnp.int16
NY, NZ, NVIR, NOCC = 4, 32, 64, 16
ROWS, DEPTH, OWN = 100, 1536, 512
MAIN, HALF, TAIL, QUART = 96, 48, 4, 384
SLOTS, MAINS, COLS = 8, 768, 896
STRIDE = 4
STEPS = 16 // STRIDE
ROUND = 12582912.0
LEAST = 1.1e-34
NT = (((1,), (1,)), ((), ()))


def kernel(
    a_hbm, i_hbm, sizes_hbm, o_ref,
    a_ref, i_ref, sizes_ref, sibling, turned, mains, tails, tail_f32, own_tail, rest_f32, rest,
    part, coded, coded_in, scale, scale_in, total, out_q, out_u, raw_q, raw_u, run_q, run_u, ends, end_in,
    ready_m, ready_t, sent, i_sem, x_sem, raw_sem, run_sem, end_sem, load_sem,
):
    occ, vir = lax.axis_index("occ"), lax.axis_index("vir")
    core = lax.rem(occ, 2)
    y = lax.rem(lax.div(occ, 2), NY)
    x_lo = lax.div(occ, 2 * NY)
    z, x_hi = lax.div(vir, 2), lax.rem(vir, 2)

    def at_y(step):
        return lax.rem(y + step + NY, NY)

    def chip(x, yy, c):
        return (x * (2 * NY) + yy * 2 + c, vir)

    def at_z(step):
        return (occ, lax.rem(vir + 2 * step + NVIR, NVIR))

    twin = chip(x_lo, y, 1 - core)
    other_x = 1 - x_lo
    partner = (occ, vir + 1 - 2 * x_hi)
    peers = [twin, partner]
    for n in range(1, STRIDE + 1):
        peers += [at_z(n), at_z(-n)]
    for c in (0, 1):
        peers += [chip(other_x, y, c), chip(x_lo, at_y(1), c), chip(x_lo, at_y(-1), c)]

    barrier = pltpu.get_barrier_semaphore()
    for peer in peers:
        pl.semaphore_signal(barrier, inc=1, device_id=peer, device_id_type=MESH)

    a_load = pltpu.make_async_copy(a_hbm, a_ref, load_sem.at[0])
    i_load = pltpu.make_async_copy(i_hbm, i_ref, load_sem.at[1])
    sizes_load = pltpu.make_async_copy(sizes_hbm, sizes_ref, load_sem.at[2])
    a_load.start()
    i_load.start()
    sizes_load.start()
    a_load.wait()
    last = a_ref[pl.ds(MAIN, TAIL), :].astype(F32)
    for q in range(4):
        tail_f32[pl.ds(TAIL * q, TAIL), :] = last[:, QUART * q : QUART * (q + 1)]
    own_tail[...] = tail_f32[...].astype(BF16)

    pl.semaphore_wait(barrier, len(peers))

    i_copy = pltpu.make_async_remote_copy(
        src_ref=i_ref, dst_ref=sibling, send_sem=i_sem.at[0], recv_sem=i_sem.at[1],
        device_id=twin, device_id_type=MESH,
    )

    def piece(k, h):
        if h == 2:
            return tails.at[k], ready_t.at[k]
        return mains.at[k, pl.ds(HALF * h, HALF)], ready_m.at[k, h]

    def own_piece(h):
        return own_tail if h == 2 else a_ref.at[pl.ds(HALF * h, HALF)]

    def send(n, src, k, h, dev):
        dst, sem = piece(k, h)
        return pltpu.make_async_remote_copy(
            src_ref=src, dst_ref=dst, send_sem=sent.at[n], recv_sem=sem,
            device_id=dev, device_id_type=MESH,
        )

    def arrived(k, h):
        dst, sem = piece(k, h)
        pltpu.make_async_remote_copy(
            src_ref=dst, dst_ref=dst, send_sem=sent.at[0], recv_sem=sem,
            device_id=twin, device_id_type=MESH,
        ).wait_recv()

    def turn(source, c):
        live = sizes_ref[vir]
        for b in range(DEPTH // 256):
            block = source[pl.ds(256 * b, 256), :].astype(F32)
            row = lax.broadcasted_iota(jnp.int32, block.shape, 0) + 256 * b
            block = jnp.where(row < live, block, 0.0)
            turned[c, :, 256 * b : 256 * (b + 1)] = block.T.astype(BF16)

    up, down, far = at_y(1), at_y(-1), at_y(2)
    shapes = {0: [], 1: []}

    def go(role, src, k, h, dev):
        copy = send(len(shapes[role]), src, k, h, dev)
        copy.start()
        shapes[role].append(h)

    def pass_on(role, k, h, dev):
        go(role, piece(k, h)[0], k, h, dev)

    def start_own(role, dests):
        for dev in dests:
            for h in range(3):
                go(role, own_piece(h), 2 * y + core, h, dev)
        i_load.wait()
        i_copy.start()

    def turn_own():
        sizes_load.wait()
        turn(i_ref, core)

    def turn_sibling():
        i_copy.wait_recv()
        turn(sibling, 1 - core)

    @pl.when(core == 0)
    def _():
        start_own(0, [chip(x_lo, up, 0), chip(x_lo, down, 0), chip(other_x, y, 1)])
        for h in range(2):
            mains[2 * y, pl.ds(HALF * h, HALF)] = a_ref[pl.ds(HALF * h, HALF), :]
        tails[2 * y] = own_tail[...]
        turn_own()
        for c in (0, 1):
            for h in (0, 2, 1):
                for src, dev, keep in ((2 * down + c, up, h != 1), (2 * up + c, down, h == 1)):
                    arrived(src, h)
                    if keep:
                        pass_on(0, src, h, chip(x_lo, dev, 0))
        turn_sibling()
        for c in (0, 1):
            for h in (0, 2, 1):
                arrived(2 * far + c, h)
                pass_on(0, 2 * far + c, h, chip(other_x, y, 1))
        for h in range(3):
            arrived(2 * y + 1, h)

    @pl.when(core == 1)
    def _():
        start_own(1, [chip(x_lo, up, 0), chip(x_lo, down, 0), chip(other_x, y, 1), chip(x_lo, y, 0)])
        turn_own()
        for c in (0, 1):
            for h in range(3):
                arrived(2 * y + c, h)
                for dev in (up, down):
                    pass_on(1, 2 * y + c, h, chip(x_lo, dev, 1))
        turn_sibling()
        for dev in (up, down, far):
            for c in (0, 1):
                for h in range(3):
                    arrived(2 * dev + c, h)

    for k in range(SLOTS):
        block = tails[k].astype(F32)
        for q in range(4):
            rest_f32[pl.ds(TAIL * k, TAIL), QUART * q : QUART * (q + 1)] = block[TAIL * q : TAIL * (q + 1), :]
    rest[pl.ds(0, 32), :] = rest_f32[...].astype(BF16)
    rest[pl.ds(32, 96), :] = jnp.zeros((96, DEPTH), BF16)

    def multiply(c, carry):
        lhs = turned[c]
        for rhs, lo, hi in ((mains[...].reshape(MAINS, DEPTH), 0, MAINS), (rest[...], MAINS, COLS)):
            out = lax.dot_general(lhs, rhs, NT, preferred_element_type=F32)
            out = out.reshape(NZ, 2, 8, hi - lo)
            for h in (0, 1):
                part[h, c, :, :, lo:hi] = out[:, h]
        return carry

    lax.fori_loop(0, 2, multiply, 0)

    def plane(i):
        far_by = 16 - lax.div(i + 1, 2)
        return lax.rem(z + jnp.where(lax.rem(i, 2) == 1, far_by, -far_by) + NZ, NZ)

    def at(step):
        return lax.rem(z + step + NZ, NZ)

    away = 1 - x_hi

    def group_copies(g):
        return [
            pltpu.make_async_remote_copy(
                src_ref=src, dst_ref=dst, send_sem=x_sem.at[0, n, g], recv_sem=x_sem.at[1, n, g],
                device_id=partner, device_id_type=MESH,
            )
            for n, (src, dst) in enumerate((
                (scale.at[g], scale_in.at[g]),
                (coded.at[pl.ds(4 * g, 4)], coded_in.at[pl.ds(4 * g, 4)]),
            ))
        ]

    def rounded(values):
        return ((values + ROUND) - ROUND).astype(jnp.int32).astype(I16)

    def encode(g, carry):
        top = jnp.zeros((8, COLS), F32)
        for n in range(4):
            for c in (0, 1):
                top = jnp.maximum(top, jnp.abs(part[away, c, plane(4 * g + n)]))
        top = jnp.maximum(jnp.max(top, axis=0, keepdims=True), LEAST)
        scale[g] = top * (1.0 / 32767.0)
        gain = 32767.0 / top
        for n in range(4):
            i = 4 * g + n
            coded[i] = rounded(jnp.concatenate([part[away, c, plane(i)] for c in (0, 1)], axis=0) * gain)
        for copy in group_copies(g):
            copy.start()
        return carry

    lax.fori_loop(0, 8, encode, 0)

    def towards(side, distance):
        return at_z(distance if side == 0 else -distance)

    def copies_of(src, dst_q, dst_u, sems, dev):
        return [
            pltpu.make_async_remote_copy(
                src_ref=a, dst_ref=b, send_sem=sems(0, n), recv_sem=sems(1, n), device_id=dev, device_id_type=MESH
            )
            for n, (a, b) in enumerate(((out_q.at[src], dst_q), (out_u.at[src], dst_u)))
        ]

    def raw_copies(side, m, j, src):
        return copies_of(
            src, raw_q.at[side, m, j], raw_u.at[side, m, j],
            lambda end, n: raw_sem.at[end, n, side, m, j], towards(side, j + 1),
        )

    def run_copies(side, m, src):
        return copies_of(
            src, run_q.at[side, m], run_u.at[side, m],
            lambda end, n: run_sem.at[end, n, side, m], towards(side, STRIDE),
        )

    def has_run(side, m):
        return not (side == 1 and m == STEPS - 1)

    def pack(here, values):
        top = jnp.maximum(jnp.max(jnp.abs(values), axis=0, keepdims=True), LEAST)
        out_u[here] = top * (1.0 / 32767.0)
        out_q[here] = rounded(values * (32767.0 / top))

    def unpack(q, u):
        return q.astype(jnp.int32).astype(F32) * u

    def start(copies):
        for copy in copies:
            copy.start()

    def finish(copies):
        for copy in copies:
            copy.wait_recv()

    def distance(i):
        far_by = 16 - (i + 1) // 2
        return far_by if i % 2 == 1 else -far_by

    def take(g):
        finish(group_copies(g))
        unit = scale_in[g]
        for n in range(4):
            k = 16 if (g, n) == (0, 0) else distance(4 * g + n)
            here = at(k)
            values = jnp.concatenate([part[x_hi, c, here] for c in (0, 1)], axis=0)
            values = values + unpack(coded_in[4 * g + n], unit)
            side, k = (0, k) if k > 0 else (1, -k)
            if k == 16:
                pack(here, values)
                start(run_copies(0, STEPS - 1, here))
            elif k % STRIDE:
                pack(here, values)
                start(raw_copies(side, k // STRIDE, k % STRIDE - 1, here))
            else:
                total[here] = values

    def step(m):
        for side in (0, 1):
            here = at(STRIDE * m if side == 0 else -STRIDE * m)
            values = total[here]
            for j in range(STRIDE - 1):
                finish(raw_copies(side, m, j, here))
                values = values + unpack(raw_q[side, m, j], raw_u[side, m, j])
            if has_run(side, m):
                finish(run_copies(side, m, here))
                values = values + unpack(run_q[side, m], run_u[side, m])
            if m > 0:
                pack(here, values)
                start(run_copies(side, m - 1, here))
            else:
                total[here] = values

    last_group = {}
    for i in range(32):
        k = abs(distance(i))
        if i > 0 and k % STRIDE == 0:
            last_group[k // STRIDE] = i // 4
    taken = 0
    for m in reversed(range(STEPS)):
        while taken < min(8, last_group[m] + 2):
            take(taken)
            taken += 1
        step(m)

    ends[0] = total[z, pl.ds(0, 8)]
    ends[1] = total[z, pl.ds(8, 8)]
    end_copy = pltpu.make_async_remote_copy(
        src_ref=ends.at[1 - core], dst_ref=end_in, send_sem=end_sem.at[0], recv_sem=end_sem.at[1],
        device_id=twin, device_id_type=MESH,
    )
    end_copy.start()
    mine = ends[core]
    end_copy.wait_recv()
    theirs = end_in[...]

    def spread(block):
        pieces = []
        for k in range(SLOTS):
            pieces.append(block[:, MAIN * k : MAIN * (k + 1)])
            pieces.append(block[:, MAINS + TAIL * k : MAINS + TAIL * (k + 1)])
        return jnp.concatenate(pieces, axis=1)

    mine, theirs = spread(mine), spread(theirs)
    first = lax.rem(core + x_lo, 2) == 0
    o_ref[...] = jnp.concatenate(
        [jnp.where(first, mine, theirs), jnp.where(first, theirs, mine)], axis=1
    )

    for role in (0, 1):

        @pl.when(core == role)
        def _(role=role):
            for n, h in enumerate(shapes[role]):
                send(n, own_piece(h), 0, h, twin).wait_send()

    i_copy.wait_send()
    sends = [group_copies(g) for g in range(8)]
    for side in (0, 1):
        for m in range(STEPS):
            sends += [raw_copies(side, m, j, 0) for j in range(STRIDE - 1)]
            if has_run(side, m):
                sends.append(run_copies(side, m, 0))
    for copies in sends:
        for copy in copies:
            copy.wait_send()
    end_copy.wait_send()


def on_device(amplitudes, integrals, block_sizes):
    hbm = pl.BlockSpec(memory_space=pltpu.HBM)
    return pl.pallas_call(
        kernel,
        out_shape=jax.ShapeDtypeStruct((8, NOCC * ROWS), F32),
        in_specs=[hbm, hbm, hbm],
        out_specs=pl.BlockSpec(memory_space=pltpu.VMEM),
        scratch_shapes=[
            pltpu.VMEM((ROWS, DEPTH), BF16),
            pltpu.VMEM((DEPTH, OWN), BF16),
            pltpu.SMEM((NVIR,), jnp.int32),
            pltpu.VMEM((DEPTH, OWN), BF16),
            pltpu.VMEM((2, OWN, DEPTH), BF16),
            pltpu.VMEM((SLOTS, MAIN, DEPTH), BF16),
            pltpu.VMEM((SLOTS, 16, QUART), BF16),
            pltpu.VMEM((16, QUART), F32),
            pltpu.VMEM((16, QUART), BF16),
            pltpu.VMEM((32, DEPTH), F32),
            pltpu.VMEM((128, DEPTH), BF16),
            pltpu.VMEM((2, 2, NZ, 8, COLS), F32),
            pltpu.VMEM((NZ, 16, COLS), I16),
            pltpu.VMEM((NZ, 16, COLS), I16),
            pltpu.VMEM((8, 1, COLS), F32),
            pltpu.VMEM((8, 1, COLS), F32),
            pltpu.VMEM((NZ, 16, COLS), F32),
            pltpu.VMEM((NZ, 16, COLS), I16),
            pltpu.VMEM((NZ, 1, COLS), F32),
            pltpu.VMEM((2, STEPS, STRIDE - 1, 16, COLS), I16),
            pltpu.VMEM((2, STEPS, STRIDE - 1, 1, COLS), F32),
            pltpu.VMEM((2, STEPS, 16, COLS), I16),
            pltpu.VMEM((2, STEPS, 1, COLS), F32),
            pltpu.VMEM((2, 8, COLS), F32),
            pltpu.VMEM((8, COLS), F32),
            pltpu.SemaphoreType.DMA((SLOTS, 2)),
            pltpu.SemaphoreType.DMA((SLOTS,)),
            pltpu.SemaphoreType.DMA((32,)),
            pltpu.SemaphoreType.DMA((2,)),
            pltpu.SemaphoreType.DMA((2, 2, 8)),
            pltpu.SemaphoreType.DMA((2, 2, 2, STEPS, STRIDE - 1)),
            pltpu.SemaphoreType.DMA((2, 2, 2, STEPS)),
            pltpu.SemaphoreType.DMA((2,)),
            pltpu.SemaphoreType.DMA((3,)),
        ],
        name="ladder",
        cost_estimate=pl.CostEstimate(
            flops=2 * 1024 * DEPTH * COLS, bytes_accessed=2 * DEPTH * (OWN + ROWS), transcendentals=0
        ),
        compiler_params=pltpu.CompilerParams(
            collective_id=0, has_side_effects=True, vmem_limit_bytes=62 * 2**20
        ),
    )(amplitudes, integrals, block_sizes)


def solution(mesh):
    in_specs = (P("occ", "vir"), P("vir", "occ"), P())
    out_specs = P(("occ", "vir"), None)
    return jax.shard_map(
        on_device, mesh=mesh, in_specs=in_specs, out_specs=out_specs, check_vma=False
    )
```

```python
import jax
import jax.numpy as jnp
from jax import lax
from jax.experimental import pallas as pl
from jax.experimental.pallas import tpu as pltpu
from jax.sharding import PartitionSpec as P

MESH = pl.DeviceIdType.MESH
F32, BF16, I16 = jnp.float32, jnp.bfloat16, jnp.int16
NY, NZ, NVIR, NOCC = 4, 32, 64, 16
ROWS, DEPTH, OWN = 100, 1536, 512
MAIN, HALF, TAIL, QUART = 96, 48, 4, 384
SLOTS, MAINS, COLS = 8, 768, 896
STRIDE = 4
STEPS = 16 // STRIDE
ROUND = 12582912.0
LEAST = 1.1e-34
NT = (((1,), (1,)), ((), ()))


def kernel(
    a_hbm, i_hbm, sizes_hbm, o_ref,
    a_ref, i_ref, sizes_ref, sibling, turned, mains, tails, tail_f32, own_tail, rest_f32, rest,
    part, coded, coded_in, scale, scale_in, total, out_q, out_u, raw_q, raw_u, run_q, run_u, ends, end_in,
    ready_m, ready_t, sent, i_sem, x_sem, raw_sem, run_sem, end_sem, load_sem,
):
    occ, vir = lax.axis_index("occ"), lax.axis_index("vir")
    core = lax.rem(occ, 2)
    y = lax.rem(lax.div(occ, 2), NY)
    x_lo = lax.div(occ, 2 * NY)
    z, x_hi = lax.div(vir, 2), lax.rem(vir, 2)

    def at_y(step):
        return lax.rem(y + step + NY, NY)

    def chip(x, yy, c):
        return (x * (2 * NY) + yy * 2 + c, vir)

    def at_z(step):
        return (occ, lax.rem(vir + 2 * step + NVIR, NVIR))

    twin = chip(x_lo, y, 1 - core)
    other_x = 1 - x_lo
    partner = (occ, vir + 1 - 2 * x_hi)
    peers = []
    for n in (STRIDE, 2, 1):
        peers += [at_z(n), at_z(-n)]
    peers.append(partner)
    for c in (0, 1):
        peers += [chip(other_x, y, c), chip(x_lo, at_y(1), c), chip(x_lo, at_y(-1), c)]
    peers.append(twin)

    barrier = pltpu.get_barrier_semaphore()
    for peer in peers:
        pl.semaphore_signal(barrier, inc=1, device_id=peer, device_id_type=MESH)

    a_load = pltpu.make_async_copy(a_hbm, a_ref, load_sem.at[0])
    i_load = pltpu.make_async_copy(i_hbm, i_ref, load_sem.at[1])
    sizes_load = pltpu.make_async_copy(sizes_hbm, sizes_ref, load_sem.at[2])
    a_load.start()
    i_load.start()
    sizes_load.start()
    a_load.wait()
    last = a_ref[pl.ds(MAIN, TAIL), :].astype(F32)
    for q in range(4):
        tail_f32[pl.ds(TAIL * q, TAIL), :] = last[:, QUART * q : QUART * (q + 1)]
    own_tail[...] = tail_f32[...].astype(BF16)

    pl.semaphore_wait(barrier, len(peers))

    i_copy = pltpu.make_async_remote_copy(
        src_ref=i_ref, dst_ref=sibling, send_sem=i_sem.at[0], recv_sem=i_sem.at[1],
        device_id=twin, device_id_type=MESH,
    )

    def piece(k, h):
        if h == 2:
            return tails.at[k], ready_t.at[k]
        return mains.at[k, pl.ds(HALF * h, HALF)], ready_m.at[k, h]

    def own_piece(h):
        return own_tail if h == 2 else a_ref.at[pl.ds(HALF * h, HALF)]

    def send(n, src, k, h, dev):
        dst, sem = piece(k, h)
        return pltpu.make_async_remote_copy(
            src_ref=src, dst_ref=dst, send_sem=sent.at[n], recv_sem=sem,
            device_id=dev, device_id_type=MESH,
        )

    def arrived(k, h):
        dst, sem = piece(k, h)
        pltpu.make_async_remote_copy(
            src_ref=dst, dst_ref=dst, send_sem=sent.at[0], recv_sem=sem,
            device_id=twin, device_id_type=MESH,
        ).wait_recv()

    def turn(source, c):
        live = sizes_ref[vir]
        for b in range(DEPTH // 256):
            block = source[pl.ds(256 * b, 256), :].astype(F32)
            row = lax.broadcasted_iota(jnp.int32, block.shape, 0) + 256 * b
            block = jnp.where(row < live, block, 0.0)
            block = block.T.reshape(NZ, 2, 8, 256)
            for h in (0, 1):
                turned[h, c, :, 256 * b : 256 * (b + 1)] = block[:, h].reshape(OWN // 2, 256).astype(BF16)

    up, down, far = at_y(1), at_y(-1), at_y(2)
    shapes = {0: [], 1: []}

    def go(role, src, k, h, dev):
        copy = send(len(shapes[role]), src, k, h, dev)
        copy.start()
        shapes[role].append(h)

    def pass_on(role, k, h, dev):
        go(role, piece(k, h)[0], k, h, dev)

    def start_own(role, dests):
        for dev in dests:
            for h in range(3):
                go(role, own_piece(h), 2 * y + core, h, dev)
        i_load.wait()
        i_copy.start()

    def turn_own():
        sizes_load.wait()
        turn(i_ref, core)

    def turn_sibling():
        i_copy.wait_recv()
        turn(sibling, 1 - core)

    @pl.when(core == 0)
    def _():
        start_own(0, [chip(x_lo, up, 0), chip(x_lo, down, 0), chip(other_x, y, 1)])
        for h in range(2):
            mains[2 * y, pl.ds(HALF * h, HALF)] = a_ref[pl.ds(HALF * h, HALF), :]
        tails[2 * y] = own_tail[...]
        turn_own()
        for c in (0, 1):
            for h in (0, 2, 1):
                for src, dev, keep in ((2 * down + c, up, h != 1), (2 * up + c, down, h == 1)):
                    arrived(src, h)
                    if keep:
                        pass_on(0, src, h, chip(x_lo, dev, 0))
        turn_sibling()
        for c in (0, 1):
            for h in (0, 2, 1):
                arrived(2 * far + c, h)
                pass_on(0, 2 * far + c, h, chip(other_x, y, 1))
        for h in range(3):
            arrived(2 * y + 1, h)

    @pl.when(core == 1)
    def _():
        start_own(1, [chip(x_lo, up, 0), chip(x_lo, down, 0), chip(other_x, y, 1), chip(x_lo, y, 0)])
        turn_own()
        for c in (0, 1):
            for h in range(3):
                arrived(2 * y + c, h)
                for dev in (up, down):
                    pass_on(1, 2 * y + c, h, chip(x_lo, dev, 1))
        turn_sibling()
        for dev in (up, down, far):
            for c in (0, 1):
                for h in range(3):
                    arrived(2 * dev + c, h)

    for k in range(SLOTS):
        block = tails[k].astype(F32)
        for q in range(4):
            rest_f32[pl.ds(TAIL * k, TAIL), QUART * q : QUART * (q + 1)] = block[TAIL * q : TAIL * (q + 1), :]
    rest[pl.ds(0, 32), :] = rest_f32[...].astype(BF16)
    rest[pl.ds(32, 96), :] = jnp.zeros((96, DEPTH), BF16)

    def multiply(h):
        lhs = turned[h].reshape(OWN, DEPTH)
        for rhs, lo, hi in ((mains[...].reshape(MAINS, DEPTH), 0, MAINS), (rest[...], MAINS, COLS)):
            out = lax.dot_general(lhs, rhs, NT, preferred_element_type=F32)
            part[h, :, :, :, lo:hi] = out.reshape(2, NZ, 8, hi - lo)

    def plane(i):
        far_by = 16 - lax.div(i + 1, 2)
        return lax.rem(z + jnp.where(lax.rem(i, 2) == 1, far_by, -far_by) + NZ, NZ)

    def at(step):
        return lax.rem(z + step + NZ, NZ)

    away = 1 - x_hi
    multiply(away)

    def group_copies(g):
        return [
            pltpu.make_async_remote_copy(
                src_ref=src, dst_ref=dst, send_sem=x_sem.at[0, n, g], recv_sem=x_sem.at[1, n, g],
                device_id=partner, device_id_type=MESH,
            )
            for n, (src, dst) in enumerate((
                (scale.at[g], scale_in.at[g]),
                (coded.at[pl.ds(4 * g, 4)], coded_in.at[pl.ds(4 * g, 4)]),
            ))
        ]

    def rounded(values):
        return ((values + ROUND) - ROUND).astype(jnp.int32).astype(I16)

    def encode(g, carry):
        top = jnp.zeros((8, COLS), F32)
        for n in range(4):
            for c in (0, 1):
                top = jnp.maximum(top, jnp.abs(part[away, c, plane(4 * g + n)]))
        top = jnp.maximum(jnp.max(top, axis=0, keepdims=True), LEAST)
        scale[g] = top * (1.0 / 32767.0)
        gain = 32767.0 / top
        for n in range(4):
            i = 4 * g + n
            coded[i] = rounded(jnp.concatenate([part[away, c, plane(i)] for c in (0, 1)], axis=0) * gain)
        for copy in group_copies(g):
            copy.start()
        return carry

    lax.fori_loop(0, 8, encode, 0)
    multiply(x_hi)

    def towards(side, distance):
        return at_z(distance if side == 0 else -distance)

    def copies_of(src, dst_q, dst_u, sems, dev):
        return [
            pltpu.make_async_remote_copy(
                src_ref=a, dst_ref=b, send_sem=sems(0, n), recv_sem=sems(1, n), device_id=dev, device_id_type=MESH
            )
            for n, (a, b) in enumerate(((out_q.at[src], dst_q), (out_u.at[src], dst_u)))
        ]

    def raw_copies(side, m, j, src):
        return copies_of(
            src, raw_q.at[side, m, j], raw_u.at[side, m, j],
            lambda end, n: raw_sem.at[end, n, side, m, j], towards(side, 2 if j == 1 else 1),
        )

    def run_copies(side, m, src):
        return copies_of(
            src, run_q.at[side, m], run_u.at[side, m],
            lambda end, n: run_sem.at[end, n, side, m], towards(side, STRIDE),
        )

    def has_run(side, m):
        return not (side == 1 and m == STEPS - 1)

    def pack(here, values):
        top = jnp.maximum(jnp.max(jnp.abs(values), axis=0, keepdims=True), LEAST)
        out_u[here] = top * (1.0 / 32767.0)
        out_q[here] = rounded(values * (32767.0 / top))

    def unpack(q, u):
        return q.astype(jnp.int32).astype(F32) * u

    def start(copies):
        for copy in copies:
            copy.start()

    def finish(copies):
        for copy in copies:
            copy.wait_recv()

    def distance(i):
        far_by = 16 - (i + 1) // 2
        return far_by if i % 2 == 1 else -far_by

    def take(g):
        finish(group_copies(g))
        unit = scale_in[g]
        for n in range(4):
            k = 16 if (g, n) == (0, 0) else distance(4 * g + n)
            here = at(k)
            values = jnp.concatenate([part[x_hi, c, here] for c in (0, 1)], axis=0)
            values = values + unpack(coded_in[4 * g + n], unit)
            side, k = (0, k) if k > 0 else (1, -k)
            if k == 16:
                pack(here, values)
                start(run_copies(0, STEPS - 1, here))
            elif k % 2:
                pack(here, values)
                start(raw_copies(side, k // STRIDE, k % STRIDE - 1, here))
            else:
                total[here] = values

    def middle(m):
        for side in (0, 1):
            k = STRIDE * m + 2
            here = at(k if side == 0 else -k)
            finish(raw_copies(side, m, 2, here))
            pack(here, total[here] + unpack(raw_q[side, m, 2], raw_u[side, m, 2]))
            start(raw_copies(side, m, 1, here))

    def step(m):
        for side in (0, 1):
            here = at(STRIDE * m if side == 0 else -STRIDE * m)
            values = total[here]
            for j in (0, 1):
                finish(raw_copies(side, m, j, here))
                values = values + unpack(raw_q[side, m, j], raw_u[side, m, j])
            if has_run(side, m):
                finish(run_copies(side, m, here))
                values = values + unpack(run_q[side, m], run_u[side, m])
            if m > 0:
                pack(here, values)
                start(run_copies(side, m - 1, here))
            else:
                total[here] = values

    for what in ("t0", "t1", "m3", "t2", "s3", "t3", "m2", "t4", "s2", "t5", "m1", "t6", "s1", "t7", "m0", "s0"):
        {"t": take, "m": middle, "s": step}[what[0]](int(what[1]))

    ends[0] = total[z, pl.ds(0, 8)]
    ends[1] = total[z, pl.ds(8, 8)]
    end_copy = pltpu.make_async_remote_copy(
        src_ref=ends.at[1 - core], dst_ref=end_in, send_sem=end_sem.at[0], recv_sem=end_sem.at[1],
        device_id=twin, device_id_type=MESH,
    )
    end_copy.start()
    mine = ends[core]
    end_copy.wait_recv()
    theirs = end_in[...]

    def spread(block):
        pieces = []
        for k in range(SLOTS):
            pieces.append(block[:, MAIN * k : MAIN * (k + 1)])
            pieces.append(block[:, MAINS + TAIL * k : MAINS + TAIL * (k + 1)])
        return jnp.concatenate(pieces, axis=1)

    mine, theirs = spread(mine), spread(theirs)
    first = lax.rem(core + x_lo, 2) == 0
    o_ref[...] = jnp.concatenate(
        [jnp.where(first, mine, theirs), jnp.where(first, theirs, mine)], axis=1
    )

    for role in (0, 1):

        @pl.when(core == role)
        def _(role=role):
            for n, h in enumerate(shapes[role]):
                send(n, own_piece(h), 0, h, twin).wait_send()

    i_copy.wait_send()
    sends = [group_copies(g) for g in range(8)]
    for side in (0, 1):
        for m in range(STEPS):
            sends += [raw_copies(side, m, j, 0) for j in range(STRIDE - 1)]
            if has_run(side, m):
                sends.append(run_copies(side, m, 0))
    for copies in sends:
        for copy in copies:
            copy.wait_send()
    end_copy.wait_send()


def on_device(amplitudes, integrals, block_sizes):
    hbm = pl.BlockSpec(memory_space=pltpu.HBM)
    return pl.pallas_call(
        kernel,
        out_shape=jax.ShapeDtypeStruct((8, NOCC * ROWS), F32),
        in_specs=[hbm, hbm, hbm],
        out_specs=pl.BlockSpec(memory_space=pltpu.VMEM),
        scratch_shapes=[
            pltpu.VMEM((ROWS, DEPTH), BF16),
            pltpu.VMEM((DEPTH, OWN), BF16),
            pltpu.SMEM((NVIR,), jnp.int32),
            pltpu.VMEM((DEPTH, OWN), BF16),
            pltpu.VMEM((2, 2, OWN // 2, DEPTH), BF16),
            pltpu.VMEM((SLOTS, MAIN, DEPTH), BF16),
            pltpu.VMEM((SLOTS, 16, QUART), BF16),
            pltpu.VMEM((16, QUART), F32),
            pltpu.VMEM((16, QUART), BF16),
            pltpu.VMEM((32, DEPTH), F32),
            pltpu.VMEM((128, DEPTH), BF16),
            pltpu.VMEM((2, 2, NZ, 8, COLS), F32),
            pltpu.VMEM((NZ, 16, COLS), I16),
            pltpu.VMEM((NZ, 16, COLS), I16),
            pltpu.VMEM((8, 1, COLS), F32),
            pltpu.VMEM((8, 1, COLS), F32),
            pltpu.VMEM((NZ, 16, COLS), F32),
            pltpu.VMEM((NZ, 16, COLS), I16),
            pltpu.VMEM((NZ, 1, COLS), F32),
            pltpu.VMEM((2, STEPS, STRIDE - 1, 16, COLS), I16),
            pltpu.VMEM((2, STEPS, STRIDE - 1, 1, COLS), F32),
            pltpu.VMEM((2, STEPS, 16, COLS), I16),
            pltpu.VMEM((2, STEPS, 1, COLS), F32),
            pltpu.VMEM((2, 8, COLS), F32),
            pltpu.VMEM((8, COLS), F32),
            pltpu.SemaphoreType.DMA((SLOTS, 2)),
            pltpu.SemaphoreType.DMA((SLOTS,)),
            pltpu.SemaphoreType.DMA((32,)),
            pltpu.SemaphoreType.DMA((2,)),
            pltpu.SemaphoreType.DMA((2, 2, 8)),
            pltpu.SemaphoreType.DMA((2, 2, 2, STEPS, STRIDE - 1)),
            pltpu.SemaphoreType.DMA((2, 2, 2, STEPS)),
            pltpu.SemaphoreType.DMA((2,)),
            pltpu.SemaphoreType.DMA((3,)),
        ],
        name="ladder",
        cost_estimate=pl.CostEstimate(
            flops=2 * 1024 * DEPTH * COLS, bytes_accessed=2 * DEPTH * (OWN + ROWS), transcendentals=0
        ),
        compiler_params=pltpu.CompilerParams(
            collective_id=0, has_side_effects=True, vmem_limit_bytes=62 * 2**20
        ),
    )(amplitudes, integrals, block_sizes)


def solution(mesh):
    in_specs = (P("occ", "vir"), P("vir", "occ"), P())
    out_specs = P(("occ", "vir"), None)
    return jax.shard_map(
        on_device, mesh=mesh, in_specs=in_specs, out_specs=out_specs, check_vma=False
    )
```

```python
import jax
import jax.numpy as jnp
from jax import lax
from jax.experimental import pallas as pl
from jax.experimental.pallas import tpu as pltpu
from jax.sharding import PartitionSpec as P

MESH = pl.DeviceIdType.MESH
F32, BF16, I16 = jnp.float32, jnp.bfloat16, jnp.int16
NY, NZ, NVIR, NOCC = 4, 32, 64, 16
ROWS, DEPTH, OWN = 100, 1536, 512
MAIN, HALF, TAIL, QUART = 96, 48, 4, 384
SLOTS, MAINS, COLS = 8, 768, 896
PER, GROUPS = 2, 16
STRIDE = 4
STEPS = 16 // STRIDE
ROUND = 12582912.0
LEAST = 1.1e-34
NT = (((1,), (1,)), ((), ()))


def kernel(
    a_hbm, i_hbm, sizes_hbm, o_ref,
    a_ref, i_ref, sizes_ref, sibling, turned, mains, tails, tail_f32, own_tail, rest_f32, rest,
    part, coded, coded_in, scale, scale_in, total, out_q, out_u, raw_q, raw_u, run_q, run_u, ends, end_in,
    ready_m, ready_t, sent, i_sem, x_sem, raw_sem, run_sem, end_sem, load_sem,
):
    occ, vir = lax.axis_index("occ"), lax.axis_index("vir")
    core = lax.rem(occ, 2)
    y = lax.rem(lax.div(occ, 2), NY)
    x_lo = lax.div(occ, 2 * NY)
    z, x_hi = lax.div(vir, 2), lax.rem(vir, 2)

    def at_y(step):
        return lax.rem(y + step + NY, NY)

    def chip(x, yy, c):
        return (x * (2 * NY) + yy * 2 + c, vir)

    def at_z(step):
        return (occ, lax.rem(vir + 2 * step + NVIR, NVIR))

    twin = chip(x_lo, y, 1 - core)
    other_x = 1 - x_lo
    partner = (occ, vir + 1 - 2 * x_hi)
    peers = []
    for n in (STRIDE, 3, 2, 1):
        peers += [at_z(n), at_z(-n)]
    peers.append(partner)
    for c in (0, 1):
        peers += [chip(other_x, y, c), chip(x_lo, at_y(1), c), chip(x_lo, at_y(-1), c)]
    peers.append(twin)

    barrier = pltpu.get_barrier_semaphore()
    for peer in peers:
        pl.semaphore_signal(barrier, inc=1, device_id=peer, device_id_type=MESH)

    a_load = pltpu.make_async_copy(a_hbm, a_ref, load_sem.at[0])
    i_load = pltpu.make_async_copy(i_hbm, i_ref, load_sem.at[1])
    sizes_load = pltpu.make_async_copy(sizes_hbm, sizes_ref, load_sem.at[2])
    a_load.start()
    i_load.start()
    sizes_load.start()
    a_load.wait()
    last = a_ref[pl.ds(MAIN, TAIL), :].astype(F32)
    for q in range(4):
        tail_f32[pl.ds(TAIL * q, TAIL), :] = last[:, QUART * q : QUART * (q + 1)]
    own_tail[...] = tail_f32[...].astype(BF16)

    pl.semaphore_wait(barrier, len(peers))

    i_copy = pltpu.make_async_remote_copy(
        src_ref=i_ref, dst_ref=sibling, send_sem=i_sem.at[0], recv_sem=i_sem.at[1],
        device_id=twin, device_id_type=MESH,
    )

    def piece(k, h):
        if h == 2:
            return tails.at[k], ready_t.at[k]
        return mains.at[k, pl.ds(HALF * h, HALF)], ready_m.at[k, h]

    def own_piece(h):
        return own_tail if h == 2 else a_ref.at[pl.ds(HALF * h, HALF)]

    def send(n, src, k, h, dev):
        dst, sem = piece(k, h)
        return pltpu.make_async_remote_copy(
            src_ref=src, dst_ref=dst, send_sem=sent.at[n], recv_sem=sem,
            device_id=dev, device_id_type=MESH,
        )

    def arrived(k, h):
        dst, sem = piece(k, h)
        pltpu.make_async_remote_copy(
            src_ref=dst, dst_ref=dst, send_sem=sent.at[0], recv_sem=sem,
            device_id=twin, device_id_type=MESH,
        ).wait_recv()

    def turn(source, c):
        live = sizes_ref[vir]
        for b in range(DEPTH // 256):
            block = source[pl.ds(256 * b, 256), :].astype(F32)
            row = lax.broadcasted_iota(jnp.int32, block.shape, 0) + 256 * b
            block = jnp.where(row < live, block, 0.0)
            block = block.T.reshape(NZ, 2, 8, 256)
            for h in (0, 1):
                turned[h, c, :, 256 * b : 256 * (b + 1)] = block[:, h].reshape(OWN // 2, 256).astype(BF16)

    up, down, far = at_y(1), at_y(-1), at_y(2)
    shapes = {0: [], 1: []}

    def go(role, src, k, h, dev):
        copy = send(len(shapes[role]), src, k, h, dev)
        copy.start()
        shapes[role].append(h)

    def pass_on(role, k, h, dev):
        go(role, piece(k, h)[0], k, h, dev)

    def start_own(role, dests):
        for dev in dests:
            for h in range(3):
                go(role, own_piece(h), 2 * y + core, h, dev)
        i_load.wait()
        i_copy.start()

    def turn_own():
        sizes_load.wait()
        turn(i_ref, core)

    def turn_sibling():
        i_copy.wait_recv()
        turn(sibling, 1 - core)

    @pl.when(core == 0)
    def _():
        start_own(0, [chip(x_lo, up, 0), chip(x_lo, down, 0), chip(other_x, y, 1)])
        for h in range(2):
            mains[2 * y, pl.ds(HALF * h, HALF)] = a_ref[pl.ds(HALF * h, HALF), :]
        tails[2 * y] = own_tail[...]
        turn_own()
        for c in (0, 1):
            for h in (0, 2, 1):
                for src, dev, keep in ((2 * down + c, up, h != 1), (2 * up + c, down, h == 1)):
                    arrived(src, h)
                    if keep:
                        pass_on(0, src, h, chip(x_lo, dev, 0))
        turn_sibling()
        for c in (0, 1):
            for h in (0, 2, 1):
                arrived(2 * far + c, h)
                pass_on(0, 2 * far + c, h, chip(other_x, y, 1))
        for h in range(3):
            arrived(2 * y + 1, h)

    @pl.when(core == 1)
    def _():
        start_own(1, [chip(x_lo, up, 0), chip(x_lo, down, 0), chip(other_x, y, 1), chip(x_lo, y, 0)])
        turn_own()
        for c in (0, 1):
            for h in range(3):
                arrived(2 * y + c, h)
                for dev in (up, down):
                    pass_on(1, 2 * y + c, h, chip(x_lo, dev, 1))
        turn_sibling()
        for dev in (up, down, far):
            for c in (0, 1):
                for h in range(3):
                    arrived(2 * dev + c, h)

    for k in range(SLOTS):
        block = tails[k].astype(F32)
        for q in range(4):
            rest_f32[pl.ds(TAIL * k, TAIL), QUART * q : QUART * (q + 1)] = block[TAIL * q : TAIL * (q + 1), :]
    rest[pl.ds(0, 32), :] = rest_f32[...].astype(BF16)
    rest[pl.ds(32, 96), :] = jnp.zeros((96, DEPTH), BF16)

    def multiply(h):
        lhs = turned[h].reshape(OWN, DEPTH)
        for rhs, lo, hi in ((mains[...].reshape(MAINS, DEPTH), 0, MAINS), (rest[...], MAINS, COLS)):
            out = lax.dot_general(lhs, rhs, NT, preferred_element_type=F32)
            part[h, :, :, :, lo:hi] = out.reshape(2, NZ, 8, hi - lo)

    def plane(i):
        far_by = 16 - lax.div(i + 1, 2)
        return lax.rem(z + jnp.where(lax.rem(i, 2) == 1, far_by, -far_by) + NZ, NZ)

    def at(step):
        return lax.rem(z + step + NZ, NZ)

    away = 1 - x_hi
    multiply(away)

    def group_copies(g):
        return [
            pltpu.make_async_remote_copy(
                src_ref=src, dst_ref=dst, send_sem=x_sem.at[0, n, g], recv_sem=x_sem.at[1, n, g],
                device_id=partner, device_id_type=MESH,
            )
            for n, (src, dst) in enumerate((
                (scale.at[g], scale_in.at[g]),
                (coded.at[pl.ds(PER * g, PER)], coded_in.at[pl.ds(PER * g, PER)]),
            ))
        ]

    def rounded(values):
        return ((values + ROUND) - ROUND).astype(jnp.int32).astype(I16)

    def encode(g, carry):
        top = jnp.zeros((8, COLS), F32)
        for n in range(PER):
            for c in (0, 1):
                top = jnp.maximum(top, jnp.abs(part[away, c, plane(PER * g + n)]))
        top = jnp.maximum(jnp.max(top, axis=0, keepdims=True), LEAST)
        scale[g] = top * (1.0 / 32767.0)
        gain = 32767.0 / top
        for n in range(PER):
            i = PER * g + n
            coded[i] = rounded(jnp.concatenate([part[away, c, plane(i)] for c in (0, 1)], axis=0) * gain)
        for copy in group_copies(g):
            copy.start()
        return carry

    lax.fori_loop(0, GROUPS, encode, 0)
    multiply(x_hi)

    def towards(side, distance):
        return at_z(distance if side == 0 else -distance)

    def copies_of(src, dst_q, dst_u, sems, dev):
        return [
            pltpu.make_async_remote_copy(
                src_ref=a, dst_ref=b, send_sem=sems(0, n), recv_sem=sems(1, n), device_id=dev, device_id_type=MESH
            )
            for n, (a, b) in enumerate(((out_q.at[src], dst_q), (out_u.at[src], dst_u)))
        ]

    def raw_copies(side, m, j, src):
        return copies_of(
            src, raw_q.at[side, m, j], raw_u.at[side, m, j],
            lambda end, n: raw_sem.at[end, n, side, m, j], towards(side, 3 if (m, j) == (3, 2) else 2 if j == 1 else 1),
        )

    def run_copies(side, m, src):
        return copies_of(
            src, run_q.at[side, m], run_u.at[side, m],
            lambda end, n: run_sem.at[end, n, side, m], towards(side, STRIDE),
        )

    def has_run(side, m):
        return not (side == 1 and m == STEPS - 1)

    def pack(here, values):
        top = jnp.maximum(jnp.max(jnp.abs(values), axis=0, keepdims=True), LEAST)
        out_u[here] = top * (1.0 / 32767.0)
        out_q[here] = rounded(values * (32767.0 / top))

    def unpack(q, u):
        return q.astype(jnp.int32).astype(F32) * u

    def start(copies):
        for copy in copies:
            copy.start()

    def finish(copies):
        for copy in copies:
            copy.wait_recv()

    def distance(i):
        far_by = 16 - (i + 1) // 2
        return far_by if i % 2 == 1 else -far_by

    def take(g):
        finish(group_copies(g))
        unit = scale_in[g]
        for n in range(PER):
            k = 16 if (g, n) == (0, 0) else distance(PER * g + n)
            here = at(k)
            values = jnp.concatenate([part[x_hi, c, here] for c in (0, 1)], axis=0)
            values = values + unpack(coded_in[PER * g + n], unit)
            side, k = (0, k) if k > 0 else (1, -k)
            if k == 16:
                pack(here, values)
                start(run_copies(0, STEPS - 1, here))
            elif k % 2 or k == 14:
                pack(here, values)
                start(raw_copies(side, k // STRIDE, k % STRIDE - 1, here))
            else:
                total[here] = values

    def middle(m):
        for side in (0, 1):
            k = STRIDE * m + 2
            here = at(k if side == 0 else -k)
            finish(raw_copies(side, m, 2, here))
            pack(here, total[here] + unpack(raw_q[side, m, 2], raw_u[side, m, 2]))
            start(raw_copies(side, m, 1, here))

    def step(m):
        for side in (0, 1):
            here = at(STRIDE * m if side == 0 else -STRIDE * m)
            values = total[here]
            for j in range(3 if m == 3 else 2):
                finish(raw_copies(side, m, j, here))
                values = values + unpack(raw_q[side, m, j], raw_u[side, m, j])
            if has_run(side, m):
                finish(run_copies(side, m, here))
                values = values + unpack(run_q[side, m], run_u[side, m])
            if m > 0:
                pack(here, values)
                start(run_copies(side, m - 1, here))
            else:
                total[here] = values

    plan = [(take, n) for n in range(GROUPS)]
    for at_group, what in ((15, (step, 0)), (15, (middle, 0)), (14, (step, 1)), (11, (middle, 1)), (10, (step, 2)), (7, (middle, 2)), (5, (step, 3))):
        plan.insert(at_group + 1, what)
    for action, n in plan:
        action(n)

    ends[0] = total[z, pl.ds(0, 8)]
    ends[1] = total[z, pl.ds(8, 8)]
    end_copy = pltpu.make_async_remote_copy(
        src_ref=ends.at[1 - core], dst_ref=end_in, send_sem=end_sem.at[0], recv_sem=end_sem.at[1],
        device_id=twin, device_id_type=MESH,
    )
    end_copy.start()
    mine = ends[core]
    end_copy.wait_recv()
    theirs = end_in[...]

    def spread(block):
        pieces = []
        for k in range(SLOTS):
            pieces.append(block[:, MAIN * k : MAIN * (k + 1)])
            pieces.append(block[:, MAINS + TAIL * k : MAINS + TAIL * (k + 1)])
        return jnp.concatenate(pieces, axis=1)

    mine, theirs = spread(mine), spread(theirs)
    first = lax.rem(core + x_lo, 2) == 0
    o_ref[...] = jnp.concatenate(
        [jnp.where(first, mine, theirs), jnp.where(first, theirs, mine)], axis=1
    )

    for role in (0, 1):

        @pl.when(core == role)
        def _(role=role):
            for n, h in enumerate(shapes[role]):
                send(n, own_piece(h), 0, h, twin).wait_send()

    i_copy.wait_send()
    sends = [group_copies(g) for g in range(GROUPS)]
    for side in (0, 1):
        for m in range(STEPS):
            sends += [raw_copies(side, m, j, 0) for j in range(STRIDE - 1)]
            if has_run(side, m):
                sends.append(run_copies(side, m, 0))
    for copies in sends:
        for copy in copies:
            copy.wait_send()
    end_copy.wait_send()


def on_device(amplitudes, integrals, block_sizes):
    hbm = pl.BlockSpec(memory_space=pltpu.HBM)
    return pl.pallas_call(
        kernel,
        out_shape=jax.ShapeDtypeStruct((8, NOCC * ROWS), F32),
        in_specs=[hbm, hbm, hbm],
        out_specs=pl.BlockSpec(memory_space=pltpu.VMEM),
        scratch_shapes=[
            pltpu.VMEM((ROWS, DEPTH), BF16),
            pltpu.VMEM((DEPTH, OWN), BF16),
            pltpu.SMEM((NVIR,), jnp.int32),
            pltpu.VMEM((DEPTH, OWN), BF16),
            pltpu.VMEM((2, 2, OWN // 2, DEPTH), BF16),
            pltpu.VMEM((SLOTS, MAIN, DEPTH), BF16),
            pltpu.VMEM((SLOTS, 16, QUART), BF16),
            pltpu.VMEM((16, QUART), F32),
            pltpu.VMEM((16, QUART), BF16),
            pltpu.VMEM((32, DEPTH), F32),
            pltpu.VMEM((128, DEPTH), BF16),
            pltpu.VMEM((2, 2, NZ, 8, COLS), F32),
            pltpu.VMEM((NZ, 16, COLS), I16),
            pltpu.VMEM((NZ, 16, COLS), I16),
            pltpu.VMEM((GROUPS, 1, COLS), F32),
            pltpu.VMEM((GROUPS, 1, COLS), F32),
            pltpu.VMEM((NZ, 16, COLS), F32),
            pltpu.VMEM((NZ, 16, COLS), I16),
            pltpu.VMEM((NZ, 1, COLS), F32),
            pltpu.VMEM((2, STEPS, STRIDE - 1, 16, COLS), I16),
            pltpu.VMEM((2, STEPS, STRIDE - 1, 1, COLS), F32),
            pltpu.VMEM((2, STEPS, 16, COLS), I16),
            pltpu.VMEM((2, STEPS, 1, COLS), F32),
            pltpu.VMEM((2, 8, COLS), F32),
            pltpu.VMEM((8, COLS), F32),
            pltpu.SemaphoreType.DMA((SLOTS, 2)),
            pltpu.SemaphoreType.DMA((SLOTS,)),
            pltpu.SemaphoreType.DMA((32,)),
            pltpu.SemaphoreType.DMA((2,)),
            pltpu.SemaphoreType.DMA((2, 2, GROUPS)),
            pltpu.SemaphoreType.DMA((2, 2, 2, STEPS, STRIDE - 1)),
            pltpu.SemaphoreType.DMA((2, 2, 2, STEPS)),
            pltpu.SemaphoreType.DMA((2,)),
            pltpu.SemaphoreType.DMA((3,)),
        ],
        name="ladder",
        cost_estimate=pl.CostEstimate(
            flops=2 * 1024 * DEPTH * COLS, bytes_accessed=2 * DEPTH * (OWN + ROWS), transcendentals=0
        ),
        compiler_params=pltpu.CompilerParams(
            collective_id=0, has_side_effects=True, vmem_limit_bytes=62 * 2**20
        ),
    )(amplitudes, integrals, block_sizes)


def solution(mesh):
    in_specs = (P("occ", "vir"), P("vir", "occ"), P())
    out_specs = P(("occ", "vir"), None)
    return jax.shard_map(
        on_device, mesh=mesh, in_specs=in_specs, out_specs=out_specs, check_vma=False
    )
```

```python
import jax
import jax.numpy as jnp
from jax import lax
from jax.experimental import pallas as pl
from jax.experimental.pallas import tpu as pltpu
from jax.sharding import PartitionSpec as P

MESH = pl.DeviceIdType.MESH
F32, BF16, I16 = jnp.float32, jnp.bfloat16, jnp.int16
NY, NZ, NVIR, NOCC = 4, 32, 64, 16
ROWS, DEPTH, OWN = 100, 1536, 512
MAIN, HALF, TAIL, QUART = 96, 48, 4, 384
SLOTS, MAINS, COLS = 8, 768, 896
PER, GROUPS = 2, 16
STRIDE = 4
STEPS = 16 // STRIDE
ROUND = 12582912.0
LEAST = 1.1e-34
NT = (((1,), (1,)), ((), ()))


def kernel(
    a_hbm, i_hbm, sizes_hbm, o_ref,
    a_ref, i_ref, sizes_ref, sibling, turned, mains, tails, tail_f32, own_tail, rest_f32, rest,
    part, coded, coded_in, scale, scale_in, total, out_q, out_u, raw_q, raw_u, run_q, run_u, ends, end_in,
    ready_m, ready_t, sent, i_sem, x_sem, raw_sem, run_sem, end_sem, load_sem,
):
    occ, vir = lax.axis_index("occ"), lax.axis_index("vir")
    core = lax.rem(occ, 2)
    y = lax.rem(lax.div(occ, 2), NY)
    x_lo = lax.div(occ, 2 * NY)
    z, x_hi = lax.div(vir, 2), lax.rem(vir, 2)

    def at_y(step):
        return lax.rem(y + step + NY, NY)

    def chip(x, yy, c):
        return (x * (2 * NY) + yy * 2 + c, vir)

    def at_z(step):
        return (occ, lax.rem(vir + 2 * step + NVIR, NVIR))

    twin = chip(x_lo, y, 1 - core)
    other_x = 1 - x_lo
    partner = (occ, vir + 1 - 2 * x_hi)
    peers = []
    for n in (STRIDE, 3, 2, 1):
        peers += [at_z(n), at_z(-n)]
    peers.append(partner)
    for c in (0, 1):
        peers += [chip(other_x, y, c), chip(x_lo, at_y(1), c), chip(x_lo, at_y(-1), c)]
    peers.append(twin)

    barrier = pltpu.get_barrier_semaphore()
    for peer in peers:
        pl.semaphore_signal(barrier, inc=1, device_id=peer, device_id_type=MESH)

    a_load = pltpu.make_async_copy(a_hbm, a_ref, load_sem.at[0])
    i_load = pltpu.make_async_copy(i_hbm, i_ref, load_sem.at[1])
    sizes_load = pltpu.make_async_copy(sizes_hbm, sizes_ref, load_sem.at[2])
    a_load.start()
    i_load.start()
    sizes_load.start()
    a_load.wait()
    last = a_ref[pl.ds(MAIN, TAIL), :].astype(F32)
    for q in range(4):
        tail_f32[pl.ds(TAIL * q, TAIL), :] = last[:, QUART * q : QUART * (q + 1)]
    own_tail[...] = tail_f32[...].astype(BF16)

    pl.semaphore_wait(barrier, len(peers))

    i_copy = pltpu.make_async_remote_copy(
        src_ref=i_ref, dst_ref=sibling, send_sem=i_sem.at[0], recv_sem=i_sem.at[1],
        device_id=twin, device_id_type=MESH,
    )

    def piece(k, h):
        if h == 2:
            return tails.at[k], ready_t.at[k]
        return mains.at[k, pl.ds(HALF * h, HALF)], ready_m.at[k, h]

    def own_piece(h):
        return own_tail if h == 2 else a_ref.at[pl.ds(HALF * h, HALF)]

    def send(n, src, k, h, dev):
        dst, sem = piece(k, h)
        return pltpu.make_async_remote_copy(
            src_ref=src, dst_ref=dst, send_sem=sent.at[n], recv_sem=sem,
            device_id=dev, device_id_type=MESH,
        )

    def arrived(k, h):
        dst, sem = piece(k, h)
        pltpu.make_async_remote_copy(
            src_ref=dst, dst_ref=dst, send_sem=sent.at[0], recv_sem=sem,
            device_id=twin, device_id_type=MESH,
        ).wait_recv()

    def turn(source, c):
        live = sizes_ref[vir]
        for b in range(DEPTH // 256):
            block = source[pl.ds(256 * b, 256), :].astype(F32)
            row = lax.broadcasted_iota(jnp.int32, block.shape, 0) + 256 * b
            block = jnp.where(row < live, block, 0.0)
            block = block.T.reshape(NZ, 2, 8, 256)
            for h in (0, 1):
                turned[h, c, :, 256 * b : 256 * (b + 1)] = block[:, h].reshape(OWN // 2, 256).astype(BF16)

    up, down, far = at_y(1), at_y(-1), at_y(2)
    shapes = {0: [], 1: []}

    def go(role, src, k, h, dev):
        copy = send(len(shapes[role]), src, k, h, dev)
        copy.start()
        shapes[role].append(h)

    def pass_on(role, k, h, dev):
        go(role, piece(k, h)[0], k, h, dev)

    def start_own(role, dests):
        for dev in dests:
            for h in range(3):
                go(role, own_piece(h), 2 * y + core, h, dev)
        i_load.wait()
        i_copy.start()

    def turn_own():
        sizes_load.wait()
        turn(i_ref, core)

    def turn_sibling():
        i_copy.wait_recv()
        turn(sibling, 1 - core)

    @pl.when(core == 0)
    def _():
        start_own(0, [chip(x_lo, up, 0), chip(x_lo, down, 0), chip(other_x, y, 1)])
        for h in range(2):
            mains[2 * y, pl.ds(HALF * h, HALF)] = a_ref[pl.ds(HALF * h, HALF), :]
        tails[2 * y] = own_tail[...]
        turn_own()
        for c in (0, 1):
            for h in (0, 2, 1):
                for src, dev, keep in ((2 * down + c, up, h != 1), (2 * up + c, down, h == 1)):
                    arrived(src, h)
                    if keep:
                        pass_on(0, src, h, chip(x_lo, dev, 0))
        turn_sibling()
        for c in (0, 1):
            for h in (0, 2, 1):
                arrived(2 * far + c, h)
                pass_on(0, 2 * far + c, h, chip(other_x, y, 1))
        for h in range(3):
            arrived(2 * y + 1, h)

    @pl.when(core == 1)
    def _():
        start_own(1, [chip(x_lo, up, 0), chip(x_lo, down, 0), chip(other_x, y, 1), chip(x_lo, y, 0)])
        turn_own()
        for c in (0, 1):
            for h in range(3):
                arrived(2 * y + c, h)
                for dev in (up, down):
                    pass_on(1, 2 * y + c, h, chip(x_lo, dev, 1))
        turn_sibling()
        for dev in (up, down, far):
            for c in (0, 1):
                for h in range(3):
                    arrived(2 * dev + c, h)

    for k in range(SLOTS):
        block = tails[k].astype(F32)
        for q in range(4):
            rest_f32[pl.ds(TAIL * k, TAIL), QUART * q : QUART * (q + 1)] = block[TAIL * q : TAIL * (q + 1), :]
    rest[pl.ds(0, 32), :] = rest_f32[...].astype(BF16)
    rest[pl.ds(32, 96), :] = jnp.zeros((96, DEPTH), BF16)

    def multiply(h):
        lhs = turned[h].reshape(OWN, DEPTH)
        for rhs, lo, hi in ((mains[...].reshape(MAINS, DEPTH), 0, MAINS), (rest[...], MAINS, COLS)):
            out = lax.dot_general(lhs, rhs, NT, preferred_element_type=F32)
            part[h, :, :, :, lo:hi] = out.reshape(2, NZ, 8, hi - lo)

    def plane(i):
        far_by = 16 - lax.div(i + 1, 2)
        return lax.rem(z + jnp.where(lax.rem(i, 2) == 1, far_by, -far_by) + NZ, NZ)

    def at(step):
        return lax.rem(z + step + NZ, NZ)

    away = 1 - x_hi
    multiply(away)

    def group_copies(g):
        return [
            pltpu.make_async_remote_copy(
                src_ref=src, dst_ref=dst, send_sem=x_sem.at[0, n, g], recv_sem=x_sem.at[1, n, g],
                device_id=partner, device_id_type=MESH,
            )
            for n, (src, dst) in enumerate((
                (scale.at[g], scale_in.at[g]),
                (coded.at[pl.ds(PER * g, PER)], coded_in.at[pl.ds(PER * g, PER)]),
            ))
        ]

    def rounded(values):
        return ((values + ROUND) - ROUND).astype(jnp.int32).astype(I16)

    def encode(g, carry):
        top = jnp.zeros((8, COLS), F32)
        for n in range(PER):
            for c in (0, 1):
                top = jnp.maximum(top, jnp.abs(part[away, c, plane(PER * g + n)]))
        top = jnp.maximum(jnp.max(top, axis=0, keepdims=True), LEAST)
        scale[g] = top * (1.0 / 32767.0)
        gain = 32767.0 / top
        for n in range(PER):
            i = PER * g + n
            coded[i] = rounded(jnp.concatenate([part[away, c, plane(i)] for c in (0, 1)], axis=0) * gain)
        for copy in group_copies(g):
            copy.start()
        return carry

    lax.fori_loop(0, GROUPS, encode, 0)
    multiply(x_hi)

    def towards(side, distance):
        return at_z(distance if side == 0 else -distance)

    def copies_of(src, dst_q, dst_u, sems, dev):
        return [
            pltpu.make_async_remote_copy(
                src_ref=a, dst_ref=b, send_sem=sems(0, n), recv_sem=sems(1, n), device_id=dev, device_id_type=MESH
            )
            for n, (a, b) in enumerate(((out_q.at[src], dst_q), (out_u.at[src], dst_u)))
        ]

    def raw_copies(side, m, j, src):
        return copies_of(
            src, raw_q.at[side, m, j], raw_u.at[side, m, j],
            lambda end, n: raw_sem.at[end, n, side, m, j], towards(side, 3 if (m, j) == (3, 2) else 2 if j == 1 else 1),
        )

    def run_copies(side, m, src):
        return copies_of(
            src, run_q.at[side, m], run_u.at[side, m],
            lambda end, n: run_sem.at[end, n, side, m], towards(side, STRIDE),
        )

    def has_run(side, m):
        return not (side == 1 and m == STEPS - 1)

    def pack(here, values):
        top = jnp.maximum(jnp.max(jnp.abs(values), axis=0, keepdims=True), LEAST)
        out_u[here] = top * (1.0 / 32767.0)
        out_q[here] = rounded(values * (32767.0 / top))

    def unpack(q, u):
        return q.astype(jnp.int32).astype(F32) * u

    def start(copies):
        for copy in copies:
            copy.start()

    def finish(copies):
        for copy in copies:
            copy.wait_recv()

    def distance(i):
        far_by = 16 - (i + 1) // 2
        return far_by if i % 2 == 1 else -far_by

    def take(g):
        finish(group_copies(g))
        unit = scale_in[g]
        for n in range(PER):
            k = 16 if (g, n) == (0, 0) else distance(PER * g + n)
            here = at(k)
            values = jnp.concatenate([part[x_hi, c, here] for c in (0, 1)], axis=0)
            values = values + unpack(coded_in[PER * g + n], unit)
            side, k = (0, k) if k > 0 else (1, -k)
            if k == 16:
                pack(here, values)
                start(run_copies(0, STEPS - 1, here))
            elif k % 2 or k == 14:
                pack(here, values)
                start(raw_copies(side, k // STRIDE, k % STRIDE - 1, here))
            else:
                total[here] = values

    def middle(m):
        for side in (0, 1):
            k = STRIDE * m + 2
            here = at(k if side == 0 else -k)
            finish(raw_copies(side, m, 2, here))
            pack(here, total[here] + unpack(raw_q[side, m, 2], raw_u[side, m, 2]))
            start(raw_copies(side, m, 1, here))

    def step(m):
        planes = [at(STRIDE * m), at(-STRIDE * m)]
        sums = []
        for side, here in enumerate(planes):
            values = total[here] if m > 0 or side == 0 else jnp.zeros((16, COLS), F32)
            for j in range(3 if m == 3 else 2):
                finish(raw_copies(side, m, j, here))
                values = values + unpack(raw_q[side, m, j], raw_u[side, m, j])
            sums.append(values)
        for side, here in enumerate(planes):
            values = sums[side]
            if has_run(side, m):
                finish(run_copies(side, m, here))
                values = values + unpack(run_q[side, m], run_u[side, m])
            if m > 0:
                pack(here, values)
                start(run_copies(side, m - 1, here))
            else:
                sums[side] = values
        if m == 0:
            total[z] = sums[0] + sums[1]

    plan = [(take, n) for n in range(GROUPS)]
    for at_group, what in ((15, (step, 0)), (15, (middle, 0)), (14, (step, 1)), (11, (middle, 1)), (10, (step, 2)), (7, (middle, 2)), (5, (step, 3))):
        plan.insert(at_group + 1, what)
    for action, n in plan:
        action(n)

    ends[0] = total[z, pl.ds(0, 8)]
    ends[1] = total[z, pl.ds(8, 8)]
    end_copy = pltpu.make_async_remote_copy(
        src_ref=ends.at[1 - core], dst_ref=end_in, send_sem=end_sem.at[0], recv_sem=end_sem.at[1],
        device_id=twin, device_id_type=MESH,
    )
    end_copy.start()
    mine = ends[core]
    end_copy.wait_recv()
    theirs = end_in[...]

    def spread(block):
        pieces = []
        for k in range(SLOTS):
            pieces.append(block[:, MAIN * k : MAIN * (k + 1)])
            pieces.append(block[:, MAINS + TAIL * k : MAINS + TAIL * (k + 1)])
        return jnp.concatenate(pieces, axis=1)

    mine, theirs = spread(mine), spread(theirs)
    first = lax.rem(core + x_lo, 2) == 0
    o_ref[...] = jnp.concatenate(
        [jnp.where(first, mine, theirs), jnp.where(first, theirs, mine)], axis=1
    )

    for role in (0, 1):

        @pl.when(core == role)
        def _(role=role):
            for n, h in enumerate(shapes[role]):
                send(n, own_piece(h), 0, h, twin).wait_send()

    i_copy.wait_send()
    sends = [group_copies(g) for g in range(GROUPS)]
    for side in (0, 1):
        for m in range(STEPS):
            sends += [raw_copies(side, m, j, 0) for j in range(STRIDE - 1)]
            if has_run(side, m):
                sends.append(run_copies(side, m, 0))
    for copies in sends:
        for copy in copies:
            copy.wait_send()
    end_copy.wait_send()


def on_device(amplitudes, integrals, block_sizes):
    hbm = pl.BlockSpec(memory_space=pltpu.HBM)
    return pl.pallas_call(
        kernel,
        out_shape=jax.ShapeDtypeStruct((8, NOCC * ROWS), F32),
        in_specs=[hbm, hbm, hbm],
        out_specs=pl.BlockSpec(memory_space=pltpu.VMEM),
        scratch_shapes=[
            pltpu.VMEM((ROWS, DEPTH), BF16),
            pltpu.VMEM((DEPTH, OWN), BF16),
            pltpu.SMEM((NVIR,), jnp.int32),
            pltpu.VMEM((DEPTH, OWN), BF16),
            pltpu.VMEM((2, 2, OWN // 2, DEPTH), BF16),
            pltpu.VMEM((SLOTS, MAIN, DEPTH), BF16),
            pltpu.VMEM((SLOTS, 16, QUART), BF16),
            pltpu.VMEM((16, QUART), F32),
            pltpu.VMEM((16, QUART), BF16),
            pltpu.VMEM((32, DEPTH), F32),
            pltpu.VMEM((128, DEPTH), BF16),
            pltpu.VMEM((2, 2, NZ, 8, COLS), F32),
            pltpu.VMEM((NZ, 16, COLS), I16),
            pltpu.VMEM((NZ, 16, COLS), I16),
            pltpu.VMEM((GROUPS, 1, COLS), F32),
            pltpu.VMEM((GROUPS, 1, COLS), F32),
            pltpu.VMEM((NZ, 16, COLS), F32),
            pltpu.VMEM((NZ, 16, COLS), I16),
            pltpu.VMEM((NZ, 1, COLS), F32),
            pltpu.VMEM((2, STEPS, STRIDE - 1, 16, COLS), I16),
            pltpu.VMEM((2, STEPS, STRIDE - 1, 1, COLS), F32),
            pltpu.VMEM((2, STEPS, 16, COLS), I16),
            pltpu.VMEM((2, STEPS, 1, COLS), F32),
            pltpu.VMEM((2, 8, COLS), F32),
            pltpu.VMEM((8, COLS), F32),
            pltpu.SemaphoreType.DMA((SLOTS, 2)),
            pltpu.SemaphoreType.DMA((SLOTS,)),
            pltpu.SemaphoreType.DMA((32,)),
            pltpu.SemaphoreType.DMA((2,)),
            pltpu.SemaphoreType.DMA((2, 2, GROUPS)),
            pltpu.SemaphoreType.DMA((2, 2, 2, STEPS, STRIDE - 1)),
            pltpu.SemaphoreType.DMA((2, 2, 2, STEPS)),
            pltpu.SemaphoreType.DMA((2,)),
            pltpu.SemaphoreType.DMA((3,)),
        ],
        name="ladder",
        cost_estimate=pl.CostEstimate(
            flops=2 * 1024 * DEPTH * COLS, bytes_accessed=2 * DEPTH * (OWN + ROWS), transcendentals=0
        ),
        compiler_params=pltpu.CompilerParams(
            collective_id=0, has_side_effects=True, vmem_limit_bytes=62 * 2**20
        ),
    )(amplitudes, integrals, block_sizes)


def solution(mesh):
    in_specs = (P("occ", "vir"), P("vir", "occ"), P())
    out_specs = P(("occ", "vir"), None)
    return jax.shard_map(
        on_device, mesh=mesh, in_specs=in_specs, out_specs=out_specs, check_vma=False
    )
```
